256 devices in a mesh: vol: 16 (over y, z_hi, core), ctl: 16 (over x, z_lo).
Axes of the slice: x: 4, y: 4, z: 8 (z_hi: 2, z_lo: 4; z = z_hi * 4 + z_lo), core: 2. Of those that a mesh axis runs over, the one named last changes fastest.
Arguments:
- vol_coords: bfloat16 [3, 65536], P(None, ('vol', 'ctl')), may hold values from 0 to 1
- vol_cotangent: bfloat16 [48, 65536], P(None, ('vol', 'ctl')), may hold values from -0.59765625 to 0.59765625
- ctl_coords: bfloat16 [3, 65536], P(None, ('ctl', 'vol')), may hold values from 0 to 1
- ctl_weights: bfloat16 [48, 65536], P(None, ('ctl', 'vol')), may hold values from -0.029907227 to 0.029907227
Outputs:
- weight_grad: float32 [48, 65536], P(None, ('ctl', 'vol'))
- vol_coord_grad: float32 [3, 65536], P(None, ('vol', 'ctl'))
- ctl_coord_grad: float32 [3, 65536], P(None, ('ctl', 'vol'))
The draws below stay inside these ranges and needn't reach their ends.
All inputs are finite; a program needn't handle non-finite values.
Results may differ from the reference program's by a relative error of at most 0.0028.
Values may be sent and summed in bfloat16 or wider, within the bound.
No kernel may reach another device: no remote copies, remote signals or barrier semaphores. Data moves between devices by JAX's collectives and lax.ppermute only.
A program may use at most 64 MiB of HBM per device.

```python
import math
import jax
import jax.numpy as jnp
from jax import lax

ROWS = 48
NVOL = 65536
NCTL = 65536


def level_of(own_key, shape, shards, low, top_value):
    loudness = 1.0
    for dim, shards_of in shards:
        steps = jax.random.uniform(jax.random.fold_in(jax.random.fold_in(own_key, 6), dim), (shards_of,), jnp.float32, low / len(shards), top_value / len(shards))
        loudness = loudness * jnp.repeat(jnp.exp(steps), shape[dim] // shards_of).reshape((-1,) + (1,) * (len(shape) - 1 - dim))
    return loudness


def noise(own_key, dims, spread, most, shards=(), held_as=jnp.bfloat16):
    result = jax.random.normal(own_key, dims, jnp.float32) * spread
    if len(shards) > 0:
        result = level_of(own_key, dims, shards, -0.22, 0.18) * result
    return jnp.clip(result, min=-most, max=most).astype(held_as)


def setup_inputs(seed: int = 0) -> dict:
    splits = jax.random.split(jax.random.key(seed), 5)
    return {
        "vol_coords": jnp.clip(1.0 * jax.random.uniform(splits[0], (3, NVOL), jnp.float32) ** level_of(splits[0], (3, NVOL), ((1, 256),), -0.2, 0.2), 0.0, 1.0).astype(jnp.bfloat16),
        "vol_cotangent": noise(splits[1], (ROWS, NVOL), 0.1, 0.59765625, ((1, 256),)),
        "ctl_coords": jnp.clip(1.0 * jax.random.uniform(splits[2], (3, NCTL), jnp.float32) ** level_of(splits[2], (3, NCTL), ((1, 256),), -0.2, 0.2), 0.0, 1.0).astype(jnp.bfloat16),
        "ctl_weights": noise(splits[3], (ROWS, NCTL), 0.005, 0.029907227, ((1, 256),)),
    }


support_radius = 0.25
slope_factor = -20.0 / (0.25 * 0.25)

def tile_terms(vol_xyz, vol_cot, ctl_xyz, ctl_wts):
    vol_pos = vol_xyz.astype(jnp.float32)
    ctl_pos = ctl_xyz.astype(jnp.float32)
    squared = jnp.zeros((vol_pos.shape[1], ctl_pos.shape[1]), jnp.float32)
    for component in range(3):
        offset = vol_pos[component][:, None] - ctl_pos[component][None, :]
        squared = squared + offset * offset
    ratio = jnp.sqrt(squared) / support_radius
    inside = jnp.maximum(1.0 - ratio, 0.0)
    cubic_term = inside * inside * inside
    kernel = (cubic_term * inside * (4.0 * ratio + 1.0)).astype(jnp.bfloat16)
    pair_dot = lax.dot_general(vol_cot, ctl_wts, (((0,), (0,)), ((), ())), preferred_element_type=jnp.float32)
    weighting = slope_factor * cubic_term * pair_dot
    weight_grad = jnp.dot(vol_cot, kernel, preferred_element_type=jnp.float32)
    row_total = lax.optimization_barrier(jnp.sum(weighting, axis=1))
    col_total = lax.optimization_barrier(jnp.sum(weighting, axis=0))
    pulled = lax.dot_general(ctl_pos, weighting, (((1,), (1,)), ((), ())), precision=lax.Precision.HIGHEST, preferred_element_type=jnp.float32)
    pushed = jnp.dot(vol_pos, weighting, precision=lax.Precision.HIGHEST, preferred_element_type=jnp.float32)
    vol_grad = vol_pos * row_total[None, :] - pulled
    ctl_grad = ctl_pos * col_total[None, :] - pushed
    return (vol_grad, weight_grad, ctl_grad)

def sweep(vol_xyz, vol_cot, ctl_xyz, ctl_wts, limit):
    vol_count = vol_xyz.shape[1]
    ctl_count = ctl_xyz.shape[1]
    block_len = math.gcd(vol_count, limit)
    blocks = vol_count // block_len
    stacked_xyz = vol_xyz.reshape(3, blocks, block_len).transpose(1, 0, 2)
    stacked_cot = vol_cot.reshape(vol_cot.shape[0], blocks, block_len).transpose(1, 0, 2)

    def advance(carry, items):
        xyz_block, cot_block = items
        vol_grad, weight_grad, ctl_grad = tile_terms(xyz_block, cot_block, ctl_xyz, ctl_wts)
        return ((carry[0] + weight_grad, carry[1] + ctl_grad), vol_grad)
    start_carry = (jnp.zeros((vol_cot.shape[0], ctl_count), jnp.float32), jnp.zeros((3, ctl_count), jnp.float32))
    totals, vol_parts = lax.scan(advance, start_carry, (stacked_xyz, stacked_cot))
    vol_grad = vol_parts.transpose(1, 0, 2).reshape(3, vol_count)
    return (vol_grad, totals[0], totals[1])

def reference(vol_coords, vol_cotangent, ctl_coords, ctl_weights):
    vol_grad, weight_grad, ctl_grad = sweep(vol_coords, vol_cotangent, ctl_coords, ctl_weights, 1024)
    return (weight_grad, vol_grad, ctl_grad)
```

```python
import jax
import jax.numpy as jnp
from jax import lax
from jax.experimental import pallas as pl
from jax.experimental.pallas import tpu as pltpu
from jax.sharding import PartitionSpec as P

F32 = jnp.float32
BF = jnp.bfloat16
VMEM = pltpu.VMEM
WIDE = 64
BLOCK = 256
SLOPE = -320.0


def split3(total):
    first = total.astype(BF)
    rest = total - first.astype(F32)
    second = rest.astype(BF)
    third = (rest - second.astype(F32)).astype(BF)
    return (first, second, third)


def pack_kernel(vx_ref, vc_ref, cx_ref, cw_ref, v_ref, c_ref):
    ones = jnp.ones((3, BLOCK), BF)
    blank = jnp.zeros((7, BLOCK), BF)
    v = vx_ref[...].astype(F32) * 4.0
    v_len = jnp.concatenate(split3(jnp.sum(v * v, axis=0, keepdims=True)), axis=0)
    v_ref[0:48, :] = vc_ref[...]
    v_ref[48:64, :] = jnp.concatenate([(v * -2.0).astype(BF), v_len, ones, blank], axis=0)
    c = cx_ref[...].astype(F32) * 4.0
    c_len = jnp.concatenate(split3(jnp.sum(c * c, axis=0, keepdims=True)), axis=0)
    c_ref[0:48, :] = cw_ref[...]
    c_ref[48:64, :] = jnp.concatenate([c.astype(BF), ones, c_len, blank], axis=0)


def pack(vol_coords, vol_cotangent, ctl_coords, ctl_weights):
    packed = jax.ShapeDtypeStruct((WIDE, BLOCK), BF)
    return pl.pallas_call(
        pack_kernel,
        out_shape=(packed, packed),
        in_specs=[pl.BlockSpec(memory_space=VMEM)] * 4,
        out_specs=[pl.BlockSpec(memory_space=VMEM)] * 2,
    )(vol_coords, vol_cotangent, ctl_coords, ctl_weights)


def pair_kernel(*refs):
    v_parts = refs[0:4]
    c_parts = refs[4:12]
    c_out, v_out, v_all, v_tall, c_all, c_two, v_sum = refs[12:]
    for part in range(4):
        for slot in range(4):
            at = (part * 4 + slot) * BLOCK
            block = v_parts[part][slot]
            v_all[:, at : at + BLOCK] = block
            v_tall[at : at + BLOCK, :] = block.T
    rows = lax.broadcasted_iota(jnp.int32, (WIDE, BLOCK), 0)
    for part in range(8):
        for slot in range(2):
            block = c_parts[part][slot]
            blank = jnp.zeros_like(block)
            c_all[part * 2 + slot] = block
            c_two[part * 2 + slot, :, :BLOCK] = jnp.where(rows >= 48, block, blank)
            c_two[part * 2 + slot, :, BLOCK:] = jnp.where(rows < 48, block, blank)
    v_sum[...] = jnp.zeros_like(v_sum)

    def tile(n, carry):
        both = jnp.dot(v_tall[...], c_two[n], preferred_element_type=F32)
        squared = jnp.maximum(both[:, :BLOCK], 1e-20)
        pair_dot = both[:, BLOCK:]
        inside = jnp.maximum(1.0 - squared * lax.rsqrt(squared), 0.0)
        second = inside * inside
        kernel = (second * second * (inside - 1.25)).astype(BF)
        weighting = (second * inside * pair_dot).astype(BF)
        weight_grad = jnp.dot(v_all[0:48, :], kernel, preferred_element_type=F32)
        pushed = jnp.dot(v_all[48:64, :], weighting, preferred_element_type=F32)
        own = c_all[n, 48:64, :]
        v_sum[...] += lax.dot_general(
            own, weighting, (((1,), (1,)), ((), ())), preferred_element_type=F32
        )
        c_out[n, 0:48, :] = weight_grad * -4.0
        ctl_pos = own[0:3].astype(F32) * 0.25
        grad = (ctl_pos * pushed[6:7] + pushed[0:3] * 0.125) * SLOPE
        c_out[n, 48:56, :] = jnp.concatenate([grad, jnp.zeros((5, BLOCK), F32)], axis=0)
        return carry

    lax.fori_loop(0, 16, tile, 0)
    for n in range(16):
        at = n * BLOCK
        pulled = v_sum[:, at : at + BLOCK]
        vol_pos = v_all[48:64, at : at + BLOCK][0:3].astype(F32) * -0.125
        grad = (vol_pos * pulled[3:4] - pulled[0:3] * 0.25) * SLOPE
        v_out[n] = jnp.concatenate([grad, jnp.zeros((5, BLOCK), F32)], axis=0)


def pair_sums(v_parts, c_parts):
    return pl.pallas_call(
        pair_kernel,
        out_shape=(
            jax.ShapeDtypeStruct((16, 56, BLOCK), F32),
            jax.ShapeDtypeStruct((16, 8, BLOCK), F32),
        ),
        in_specs=[pl.BlockSpec(memory_space=VMEM)] * 12,
        out_specs=[pl.BlockSpec(memory_space=VMEM)] * 2,
        scratch_shapes=[
            VMEM((WIDE, 16 * BLOCK), BF),
            VMEM((16 * BLOCK, WIDE), BF),
            VMEM((16, WIDE, BLOCK), BF),
            VMEM((16, WIDE, 2 * BLOCK), BF),
            VMEM((16, 16 * BLOCK), F32),
        ],
        compiler_params=pltpu.CompilerParams(vmem_limit_bytes=48 * 2**20),
        cost_estimate=pl.CostEstimate(flops=10**10, bytes_accessed=4 * 10**6, transcendentals=0),
    )(*v_parts, *c_parts)


def send(value, axis, target):
    return lax.ppermute(value, axis, [(i, target(i)) for i in range(16)])


def near(step):
    return lambda i: i // 4 * 4 + (i + step) % 4


def far(step):
    return lambda i: (i + 4 * step) % 16


def shards(vol_coords, vol_cotangent, ctl_coords, ctl_weights):
    v, c = pack(vol_coords, vol_cotangent, ctl_coords, ctl_weights)
    core = lambda i: i ^ 1
    half = lambda i: i ^ 2
    v_line = jnp.stack([v] + [send(v, "ctl", near(s)) for s in (1, 2, 3)])
    c_pair = jnp.stack([c, send(c, "vol", half)])
    v_parts = [v_line] + [send(v_line, "ctl", far(s)) for s in (1, 2, 3)]
    c_parts = [c_pair] + [send(c_pair, "vol", far(s)) for s in (1, 2, 3)]
    c_parts = c_parts + [send(part, "vol", core) for part in c_parts]
    c_out, v_out = pair_sums(v_parts, c_parts)
    c_sum = c_out[:8] + send(c_out[8:], "vol", core)
    c_back = [send(c_sum[2 * s : 2 * s + 2], "vol", far(-s)) for s in (1, 2, 3)]
    v_back = [send(v_out[4 * s : 4 * s + 4], "ctl", far(-s)) for s in (1, 2, 3)]
    c_sum = c_sum[:2] + c_back[0] + c_back[1] + c_back[2]
    v_sum = v_out[:4] + v_back[0] + v_back[1] + v_back[2]
    c_sum = c_sum[0] + send(c_sum[1], "vol", half)
    v_last = [send(v_sum[s], "ctl", near(-s)) for s in (1, 2, 3)]
    v_sum = v_sum[0] + v_last[0] + v_last[1] + v_last[2]
    return (c_sum[0:48], v_sum[0:3], c_sum[48:51])


def solution(mesh):
    in_specs = (
        P(None, ("vol", "ctl")),
        P(None, ("vol", "ctl")),
        P(None, ("ctl", "vol")),
        P(None, ("ctl", "vol")),
    )
    out_specs = (P(None, ("ctl", "vol")), P(None, ("vol", "ctl")), P(None, ("ctl", "vol")))
    return jax.shard_map(shards, mesh=mesh, in_specs=in_specs, out_specs=out_specs, check_vma=False)
```

```python
import functools

import jax
import jax.numpy as jnp
from jax import lax
from jax.experimental import pallas as pl
from jax.experimental.pallas import tpu as pltpu
from jax.sharding import PartitionSpec as P

F32 = jnp.float32
BF = jnp.bfloat16
VMEM = pltpu.VMEM
WIDE = 64
BLOCK = 256
SLOPE = -320.0


def split3(total):
    first = total.astype(BF)
    rest = total - first.astype(F32)
    second = rest.astype(BF)
    third = (rest - second.astype(F32)).astype(BF)
    return (first, second, third)


def pack_kernel(vx_ref, vc_ref, cx_ref, cw_ref, v_ref, c_ref):
    ones = jnp.ones((3, BLOCK), BF)
    blank = jnp.zeros((7, BLOCK), BF)
    v = vx_ref[...].astype(F32) * 4.0
    v_len = jnp.concatenate(split3(jnp.sum(v * v, axis=0, keepdims=True)), axis=0)
    v_ref[0, 0:48, :] = vc_ref[...]
    v_ref[0, 48:64, :] = jnp.concatenate([(v * -2.0).astype(BF), v_len, ones, blank], axis=0)
    c = cx_ref[...].astype(F32) * 4.0
    c_len = jnp.concatenate(split3(jnp.sum(c * c, axis=0, keepdims=True)), axis=0)
    c_ref[0, 0:48, :] = cw_ref[...]
    c_ref[0, 48:64, :] = jnp.concatenate([c.astype(BF), ones, c_len, blank], axis=0)


def pack(vol_coords, vol_cotangent, ctl_coords, ctl_weights):
    packed = jax.ShapeDtypeStruct((1, WIDE, BLOCK), BF)
    return pl.pallas_call(
        pack_kernel,
        out_shape=(packed, packed),
        in_specs=[pl.BlockSpec(memory_space=VMEM)] * 4,
        out_specs=[pl.BlockSpec(memory_space=VMEM)] * 2,
    )(vol_coords, vol_cotangent, ctl_coords, ctl_weights)


def pair_kernel(unroll, v_spans, c_begin, v_begin, *refs):
    refs = list(refs)
    v_parts = [refs.pop(0) for _ in v_spans]
    c_parts = [refs.pop(0) for _ in c_begin]
    c_starts = [refs.pop(0) if begin else None for begin in c_begin]
    v_starts = [refs.pop(0) if begin else None for begin in v_begin]
    c_outs = [refs.pop(0) for _ in c_begin]
    v_outs = [refs.pop(0) for _ in v_spans]
    v_all, v_tall, c_two, v_sum = refs
    at = 0
    for part, (low, high) in zip(v_parts, v_spans):
        for slot in range(low, high):
            block = part[slot]
            v_all[:, at : at + BLOCK] = block
            v_tall[at : at + BLOCK, :] = block.T
            at += BLOCK
    rows = lax.broadcasted_iota(jnp.int32, (WIDE, BLOCK), 0)
    for p, part in enumerate(c_parts):
        for slot in range(4):
            block = part[slot]
            blank = jnp.zeros_like(block)
            c_two[4 * p + slot, :, :BLOCK] = jnp.where(rows >= 48, block, blank)
            c_two[4 * p + slot, :, BLOCK:] = jnp.where(rows < 48, block, blank)
    v_sum[...] = jnp.zeros_like(v_sum)

    def tile(p, n, carry):
        both = jnp.dot(v_tall[...], c_two[4 * p + n], preferred_element_type=F32)
        squared = jnp.maximum(both[:, :BLOCK], 1e-20)
        pair_dot = both[:, BLOCK:]
        inside = jnp.maximum(1.0 - squared * lax.rsqrt(squared), 0.0)
        second = inside * inside
        kernel = (second * second * (inside - 1.25)).astype(BF)
        weighting = (second * inside * pair_dot).astype(BF)
        weight_grad = jnp.dot(v_all[0:48, :], kernel, preferred_element_type=F32)
        pushed = jnp.dot(v_all[48:64, :], weighting, preferred_element_type=F32)
        own = c_parts[p][n, 48:64, :]
        v_sum[...] += lax.dot_general(
            own, weighting, (((1,), (1,)), ((), ())), preferred_element_type=F32
        )
        ctl_pos = own[0:3].astype(F32) * 0.25
        grad = (ctl_pos * pushed[6:7] + pushed[0:3] * 0.125) * SLOPE
        found = jnp.concatenate([weight_grad * -4.0, grad, jnp.zeros((5, BLOCK), F32)], axis=0)
        start = c_starts[p]
        c_outs[p][n] = found if start is None else found + start[n]
        return carry

    for p in range(len(c_parts)):
        lax.fori_loop(0, 4, functools.partial(tile, p), 0, unroll=unroll)
    at = 0
    for part, start, (low, high) in zip(v_outs, v_starts, v_spans):
        for slot in range(high - low):
            pulled = v_sum[:, at : at + BLOCK]
            vol_pos = v_all[48:64, at : at + BLOCK][0:3].astype(F32) * -0.125
            grad = (vol_pos * pulled[3:4] - pulled[0:3] * 0.25) * SLOPE
            found = jnp.concatenate([grad, jnp.zeros((5, BLOCK), F32)], axis=0)
            part[slot] = found if start is None else found + start[slot]
            at += BLOCK


def pair_sums(v_parts, c_parts, c_starts=None, v_starts=None):
    c_starts = c_starts or [None] * len(c_parts)
    v_starts = v_starts or [None] * len(v_parts)
    v_spans = [span for _, span in v_parts]
    v_count = 4 * len(v_parts)
    c_count = 4 * len(c_parts)
    extra = [start for start in [*c_starts, *v_starts] if start is not None]
    args = [part for part, _ in v_parts] + list(c_parts) + extra
    body = functools.partial(
        pair_kernel,
        max(1, 16 // v_count),
        v_spans,
        [start is not None for start in c_starts],
        [start is not None for start in v_starts],
    )
    outs = pl.pallas_call(
        body,
        out_shape=[jax.ShapeDtypeStruct((4, 56, BLOCK), F32)] * len(c_parts)
        + [jax.ShapeDtypeStruct((4, 8, BLOCK), F32)] * len(v_parts),
        in_specs=[pl.BlockSpec(memory_space=VMEM)] * len(args),
        out_specs=[pl.BlockSpec(memory_space=VMEM)] * (len(c_parts) + len(v_parts)),
        scratch_shapes=[
            VMEM((WIDE, v_count * BLOCK), BF),
            VMEM((v_count * BLOCK, WIDE), BF),
            VMEM((c_count, WIDE, 2 * BLOCK), BF),
            VMEM((16, v_count * BLOCK), F32),
        ],
        compiler_params=pltpu.CompilerParams(vmem_limit_bytes=48 * 2**20),
        cost_estimate=pl.CostEstimate(
            flops=v_count * c_count * 2 * 10**8, bytes_accessed=4 * 10**6, transcendentals=0
        ),
    )(*args)
    return outs[: len(c_parts)], outs[len(c_parts) :]


def swap(value, mask):
    return lax.ppermute(value, ("vol", "ctl"), [(i, i ^ mask) for i in range(256)])


def gather(value, masks):
    return jnp.concatenate([value] + [swap(value, mask) for mask in masks], axis=0)


def scatter(value, masks):
    return [value[:1]] + [swap(value[s + 1 : s + 2], mask) for s, mask in enumerate(masks)]


def tie(*values):
    return lax.optimization_barrier(values)


def finish_kernel(c0, c1, c2, c3, v0, v1, v2, v3, w_ref, v_ref, c_ref):
    w_ref[...] = (c0[0, 0:48] + c1[0, 0:48]) + (c2[0, 0:48] + c3[0, 0:48])
    c_ref[...] = (c0[0, 48:51] + c1[0, 48:51]) + (c2[0, 48:51] + c3[0, 48:51])
    v_ref[...] = (v0[0, 0:3] + v1[0, 0:3]) + (v2[0, 0:3] + v3[0, 0:3])


def finish(c_terms, v_terms):
    narrow = jax.ShapeDtypeStruct((3, BLOCK), F32)
    return pl.pallas_call(
        finish_kernel,
        out_shape=(jax.ShapeDtypeStruct((48, BLOCK), F32), narrow, narrow),
        in_specs=[pl.BlockSpec(memory_space=VMEM)] * 8,
        out_specs=[pl.BlockSpec(memory_space=VMEM)] * 3,
    )(*c_terms, *v_terms)


X_MASKS = (4, 12, 8)
Y_MASKS = (64, 192, 128)
CORE, Z_ONE, Z_TWO, Z_SIX = (16, 1, 2, 34)


def shards(vol_coords, vol_cotangent, ctl_coords, ctl_weights):
    v, c = pack(vol_coords, vol_cotangent, ctl_coords, ctl_weights)
    cp, va = tie(gather(c, Y_MASKS), gather(v, X_MASKS))
    cq = swap(cp, CORE)
    cr = swap(cp, Z_ONE)
    vb = swap(va, Z_TWO)
    a = (va, (0, 4))
    (p, q), (sum_a,) = pair_sums([a], [cp, cq])
    cr, vb, p = tie(cr, vb, p)
    b = (vb, (0, 4))
    v_far = swap(jnp.concatenate([va, vb], axis=0), Z_SIX)
    c, d = ((v_far, (0, 4)), (v_far, (4, 8)))
    cs = swap(cr, CORE)
    (r,), (sum_a, sum_b) = pair_sums([a, b], [cr], None, [sum_a, None])
    (p, q), (sum_b,) = pair_sums([b], [cp, cq], [p, q], [sum_b])
    (s,), (sum_a, sum_b, sum_c, sum_d) = pair_sums(
        [a, b, c, d], [cs], None, [sum_a, sum_b, None, None]
    )
    s_back = swap(s, CORE)
    (r,), (sum_c, sum_d) = pair_sums([c, d], [cr], [r], [sum_c, sum_d])
    r = r + s_back
    r_back = swap(r, Z_ONE)
    r, q = tie(r, q)
    (q,), (sum_c, sum_d) = pair_sums([c, d], [cq], [q], [sum_c, sum_d])
    q_back = swap(q, CORE)
    (p,), (sum_d,) = pair_sums([d], [cp], [p], [sum_d])
    bd_back = swap(jnp.concatenate([sum_b, sum_d], axis=0), Z_TWO)
    (p,), (sum_c,) = pair_sums([c], [cp], [p], [sum_c])
    p, sum_c, bd_back, q_back, r_back = tie(p, sum_c, bd_back, q_back, r_back)
    sum_a = sum_a + bd_back[:4] + swap(sum_c + bd_back[4:], Z_SIX)
    c_terms = scatter(p + q_back + r_back, Y_MASKS)
    weight_grad, vol_grad, ctl_grad = finish(c_terms, scatter(sum_a, X_MASKS))
    return (weight_grad, vol_grad, ctl_grad)


def solution(mesh):
    in_specs = (
        P(None, ("vol", "ctl")),
        P(None, ("vol", "ctl")),
        P(None, ("ctl", "vol")),
        P(None, ("ctl", "vol")),
    )
    out_specs = (P(None, ("ctl", "vol")), P(None, ("vol", "ctl")), P(None, ("ctl", "vol")))
    return jax.shard_map(shards, mesh=mesh, in_specs=in_specs, out_specs=out_specs, check_vma=False)
```

```python
import functools

import jax
import jax.numpy as jnp
from jax import lax
from jax.experimental import pallas as pl
from jax.experimental.pallas import tpu as pltpu
from jax.sharding import PartitionSpec as P

F32 = jnp.float32
BF = jnp.bfloat16
VMEM = pltpu.VMEM
WIDE = 64
BLOCK = 256
SLOPE = -320.0


def split3(total):
    first = total.astype(BF)
    rest = total - first.astype(F32)
    second = rest.astype(BF)
    third = (rest - second.astype(F32)).astype(BF)
    return (first, second, third)


def pack_kernel(vx_ref, vc_ref, cx_ref, cw_ref, v_ref, c_ref):
    ones = jnp.ones((3, BLOCK), BF)
    blank = jnp.zeros((7, BLOCK), BF)
    v = vx_ref[...].astype(F32) * 4.0
    v_len = jnp.concatenate(split3(jnp.sum(v * v, axis=0, keepdims=True)), axis=0)
    v_ref[0, 0:48, :] = vc_ref[...]
    v_ref[0, 48:64, :] = jnp.concatenate([(v * -2.0).astype(BF), v_len, ones, blank], axis=0)
    c = cx_ref[...].astype(F32) * 4.0
    c_len = jnp.concatenate(split3(jnp.sum(c * c, axis=0, keepdims=True)), axis=0)
    c_ref[0, 0:48, :] = cw_ref[...]
    c_ref[0, 48:64, :] = jnp.concatenate([c.astype(BF), ones, c_len, blank], axis=0)


def pack(vol_coords, vol_cotangent, ctl_coords, ctl_weights):
    packed = jax.ShapeDtypeStruct((1, WIDE, BLOCK), BF)
    return pl.pallas_call(
        pack_kernel,
        out_shape=(packed, packed),
        in_specs=[pl.BlockSpec(memory_space=VMEM)] * 4,
        out_specs=[pl.BlockSpec(memory_space=VMEM)] * 2,
    )(vol_coords, vol_cotangent, ctl_coords, ctl_weights)


def pair_kernel(unroll, v_lows, c_lows, c_begins, v_begin, *refs):
    refs = list(refs)
    v_parts = [refs.pop(0) for _ in v_lows]
    c_parts = [refs.pop(0) for _ in c_lows]
    c_starts = [refs.pop(0) for _ in c_begins]
    v_starts = [refs.pop(0) if begin else None for begin in v_begin]
    c_out = refs.pop(0)
    v_outs = [refs.pop(0) for _ in v_lows]
    v_all, v_tall, c_two, c_pos, v_sum = refs
    at = 0
    for part, low in zip(v_parts, v_lows):
        for slot in range(4):
            block = part[low + slot]
            v_all[:, at : at + BLOCK] = block
            v_tall[at : at + BLOCK, :] = block.T
            at += BLOCK
    rows = lax.broadcasted_iota(jnp.int32, (WIDE, BLOCK), 0)
    count = 0
    for part, low in zip(c_parts, c_lows):
        for slot in range(4):
            block = part[low + slot]
            blank = jnp.zeros_like(block)
            c_two[count, :, :BLOCK] = jnp.where(rows >= 48, block, blank)
            c_two[count, :, BLOCK:] = jnp.where(rows < 48, block, blank)
            c_pos[count] = block[48:64]
            count += 1
    v_sum[...] = jnp.zeros_like(v_sum)

    def tile(n, carry):
        both = jnp.dot(v_tall[...], c_two[n], preferred_element_type=F32)
        squared = jnp.maximum(both[:, :BLOCK], 1e-20)
        pair_dot = both[:, BLOCK:]
        inside = jnp.maximum(1.0 - squared * lax.rsqrt(squared), 0.0)
        second = inside * inside
        kernel = (second * second * (inside - 1.25)).astype(BF)
        weighting = (second * inside * pair_dot).astype(BF)
        weight_grad = jnp.dot(v_all[0:48, :], kernel, preferred_element_type=F32)
        pushed = jnp.dot(v_all[48:64, :], weighting, preferred_element_type=F32)
        own = c_pos[n]
        v_sum[...] += lax.dot_general(
            own, weighting, (((1,), (1,)), ((), ())), preferred_element_type=F32
        )
        ctl_pos = own[0:3].astype(F32) * 0.25
        grad = (ctl_pos * pushed[6:7] + pushed[0:3] * 0.125) * SLOPE
        found = jnp.concatenate([weight_grad * -4.0, grad, jnp.zeros((5, BLOCK), F32)], axis=0)
        for start, begin in zip(c_starts, c_begins):
            found = found + start[begin + n]
        c_out[n] = found
        return carry

    lax.fori_loop(0, count, tile, 0, unroll=unroll)
    at = 0
    for part, start in zip(v_outs, v_starts):
        for slot in range(4):
            pulled = v_sum[:, at : at + BLOCK]
            vol_pos = v_all[48:64, at : at + BLOCK][0:3].astype(F32) * -0.125
            grad = (vol_pos * pulled[3:4] - pulled[0:3] * 0.25) * SLOPE
            found = jnp.concatenate([grad, jnp.zeros((5, BLOCK), F32)], axis=0)
            part[slot] = found if start is None else found + start[slot]
            at += BLOCK


def pair_sums(v_parts, c_parts, v_starts, c_starts=()):
    v_count = 4 * len(v_parts)
    c_count = 4 * len(c_parts)
    extra = [start for start, _ in c_starts] + [start for start in v_starts if start is not None]
    args = [part for part, _ in [*v_parts, *c_parts]] + extra
    body = functools.partial(
        pair_kernel,
        max(1, UNROLL // v_count),
        [low for _, low in v_parts],
        [low for _, low in c_parts],
        [begin for _, begin in c_starts],
        [start is not None for start in v_starts],
    )
    outs = pl.pallas_call(
        body,
        out_shape=[jax.ShapeDtypeStruct((c_count, 56, BLOCK), F32)]
        + [jax.ShapeDtypeStruct((4, 8, BLOCK), F32)] * len(v_parts),
        in_specs=[pl.BlockSpec(memory_space=VMEM)] * len(args),
        out_specs=[pl.BlockSpec(memory_space=VMEM)] * (1 + len(v_parts)),
        scratch_shapes=[
            VMEM((WIDE, v_count * BLOCK), BF),
            VMEM((v_count * BLOCK, WIDE), BF),
            VMEM((c_count, WIDE, 2 * BLOCK), BF),
            VMEM((c_count, 16, BLOCK), BF),
            VMEM((16, v_count * BLOCK), F32),
        ],
        compiler_params=pltpu.CompilerParams(vmem_limit_bytes=48 * 2**20),
        cost_estimate=pl.CostEstimate(
            flops=v_count * c_count * 2 * 10**8, bytes_accessed=4 * 10**6, transcendentals=0
        ),
    )(*args)
    return outs


def swap(value, mask):
    return lax.ppermute(value, ("vol", "ctl"), [(i, i ^ mask) for i in range(256)])


def gather(value, masks):
    return jnp.concatenate([value] + [swap(value, mask) for mask in masks], axis=0)


def back(value, masks):
    return [swap(value[s + 1], mask) for s, mask in enumerate(masks)]


def tie(*values):
    return lax.optimization_barrier(values)


UNROLL = 8
X_MASKS = (4, 12, 8)
Y_MASKS = (64, 192, 128)
CORE, Z_ONE, Z_TWO, Z_SIX = (16, 1, 2, 34)


def shards(vol_coords, vol_cotangent, ctl_coords, ctl_weights):
    v, c = pack(vol_coords, vol_cotangent, ctl_coords, ctl_weights)
    cp, va = tie(gather(c, Y_MASKS), gather(v, X_MASKS))
    cq = swap(cp, CORE)
    cr = swap(cp, Z_ONE)
    vb = swap(va, Z_TWO)
    a = (va, 0)
    pq, sum_a = pair_sums([a], [(cp, 0), (cq, 0)], [None])
    cr, vb, pq = tie(cr, vb, pq)
    b = (vb, 0)
    v_far = swap(jnp.concatenate([va, vb], axis=0), Z_SIX)
    c, d = ((v_far, 0), (v_far, 4))
    cs = swap(cr, CORE)
    pqr, sum_b = pair_sums([b], [(cp, 0), (cq, 0), (cr, 0)], [None])
    s, sum_a, sum_b, sum_c, sum_d = pair_sums(
        [a, b, c, d], [(cs, 0)], [sum_a, sum_b, None, None]
    )
    s_back = swap(s, CORE)
    r, sum_a, sum_c, sum_d = pair_sums([a, c, d], [(cr, 0)], [sum_a, sum_c, sum_d], [(pqr, 8)])
    r = r + s_back
    r_back = swap(r, Z_ONE)
    r, pq = tie(r, pq)
    q, sum_c, sum_d = pair_sums([c, d], [(cq, 0)], [sum_c, sum_d], [(pq, 4), (pqr, 4)])
    q_back = swap(q, CORE)
    p, sum_d = pair_sums([d], [(cp, 0)], [sum_d], [(pq, 0), (pqr, 0)])
    bd_back = swap(jnp.concatenate([sum_b, sum_d], axis=0), Z_TWO)
    p, sum_c = pair_sums([c], [(cp, 0)], [sum_c], [(p, 0)])
    p, sum_c, bd_back, q_back, r_back = tie(p, sum_c, bd_back, q_back, r_back)
    p = p + q_back + r_back
    ctl_0, (ctl_1, ctl_2, ctl_3), sum_a, sum_c = tie(
        p[0],
        back(p, Y_MASKS),
        sum_a + bd_back[:4],
        swap(sum_c + bd_back[4:], Z_SIX),
    )
    vol = sum_a + sum_c
    vol_1, vol_2, vol_3 = back(vol, X_MASKS)
    ctl = (ctl_0 + ctl_1) + (ctl_2 + ctl_3)
    vol = (vol[0] + vol_1) + (vol_2 + vol_3)
    return (ctl[0:48], vol[0:3], ctl[48:51])


def solution(mesh):
    in_specs = (
        P(None, ("vol", "ctl")),
        P(None, ("vol", "ctl")),
        P(None, ("ctl", "vol")),
        P(None, ("ctl", "vol")),
    )
    out_specs = (P(None, ("ctl", "vol")), P(None, ("vol", "ctl")), P(None, ("ctl", "vol")))
    return jax.shard_map(shards, mesh=mesh, in_specs=in_specs, out_specs=out_specs, check_vma=False)
```

```python
import functools

import jax
import jax.numpy as jnp
from jax import lax
from jax.experimental import pallas as pl
from jax.experimental.pallas import tpu as pltpu
from jax.sharding import PartitionSpec as P

F32 = jnp.float32
BF = jnp.bfloat16
VMEM = pltpu.VMEM
WIDE = 64
BLOCK = 256
SLOPE = -320.0


def split3(total):
    first = total.astype(BF)
    rest = total - first.astype(F32)
    second = rest.astype(BF)
    third = (rest - second.astype(F32)).astype(BF)
    return (first, second, third)


def pack_kernel(vx_ref, vc_ref, cx_ref, cw_ref, v_ref, c_ref):
    ones = jnp.ones((3, BLOCK), BF)
    blank = jnp.zeros((7, BLOCK), BF)
    v = vx_ref[...].astype(F32) * 4.0
    v_len = jnp.concatenate(split3(jnp.sum(v * v, axis=0, keepdims=True)), axis=0)
    v_ref[0, 0:48, :] = vc_ref[...]
    v_ref[0, 48:64, :] = jnp.concatenate([(v * -2.0).astype(BF), v_len, ones, blank], axis=0)
    c = cx_ref[...].astype(F32) * 4.0
    c_len = jnp.concatenate(split3(jnp.sum(c * c, axis=0, keepdims=True)), axis=0)
    c_ref[0, 0:48, :] = cw_ref[...]
    c_ref[0, 48:64, :] = jnp.concatenate([c.astype(BF), ones, c_len, blank], axis=0)


def pack(vol_coords, vol_cotangent, ctl_coords, ctl_weights):
    packed = jax.ShapeDtypeStruct((1, WIDE, BLOCK), BF)
    return pl.pallas_call(
        pack_kernel,
        out_shape=(packed, packed),
        in_specs=[pl.BlockSpec(memory_space=VMEM)] * 4,
        out_specs=[pl.BlockSpec(memory_space=VMEM)] * 2,
    )(vol_coords, vol_cotangent, ctl_coords, ctl_weights)


def pair_kernel(unroll, v_lows, c_lows, c_begins, v_begin, *refs):
    refs = list(refs)
    v_parts = [refs.pop(0) for _ in v_lows]
    c_parts = [refs.pop(0) for _ in c_lows]
    c_starts = [refs.pop(0) for _ in c_begins]
    v_starts = [refs.pop(0) if begin else None for begin in v_begin]
    c_out = refs.pop(0)
    v_outs = [refs.pop(0) for _ in v_lows]
    v_all, v_tall, c_two, c_pos, v_sum = refs
    at = 0
    for part, low in zip(v_parts, v_lows):
        for slot in range(4):
            block = part[low + slot]
            v_all[:, at : at + BLOCK] = block
            v_tall[at : at + BLOCK, :] = block.T
            at += BLOCK
    rows = lax.broadcasted_iota(jnp.int32, (WIDE, BLOCK), 0)
    count = 0
    for part, low in zip(c_parts, c_lows):
        for slot in range(4):
            block = part[low + slot]
            blank = jnp.zeros_like(block)
            c_two[count, :, :BLOCK] = jnp.where(rows >= 48, block, blank)
            c_two[count, :, BLOCK:] = jnp.where(rows < 48, block, blank)
            c_pos[count] = block[48:64]
            count += 1
    v_sum[...] = jnp.zeros_like(v_sum)

    def tile(n, carry):
        both = jnp.dot(v_tall[...], c_two[n], preferred_element_type=F32)
        squared = jnp.maximum(both[:, :BLOCK], 1e-20)
        pair_dot = both[:, BLOCK:]
        inside = jnp.maximum(1.0 - squared * lax.rsqrt(squared), 0.0)
        second = inside * inside
        kernel = (second * second * (inside - 1.25)).astype(BF)
        weighting = (second * inside * pair_dot).astype(BF)
        weight_grad = jnp.dot(v_all[0:48, :], kernel, preferred_element_type=F32)
        pushed = jnp.dot(v_all[48:64, :], weighting, preferred_element_type=F32)
        own = c_pos[n]
        v_sum[...] += lax.dot_general(
            own, weighting, (((1,), (1,)), ((), ())), preferred_element_type=F32
        )
        ctl_pos = own[0:3].astype(F32) * 0.25
        grad = (ctl_pos * pushed[6:7] + pushed[0:3] * 0.125) * SLOPE
        found = jnp.concatenate([weight_grad * -4.0, grad, jnp.zeros((5, BLOCK), F32)], axis=0)
        for start, begin in zip(c_starts, c_begins):
            found = found + start[begin + n]
        c_out[n] = found
        return carry

    lax.fori_loop(0, count, tile, 0, unroll=unroll)
    at = 0
    for part, start in zip(v_outs, v_starts):
        for slot in range(4):
            pulled = v_sum[:, at : at + BLOCK]
            vol_pos = v_all[48:64, at : at + BLOCK][0:3].astype(F32) * -0.125
            grad = (vol_pos * pulled[3:4] - pulled[0:3] * 0.25) * SLOPE
            found = jnp.concatenate([grad, jnp.zeros((5, BLOCK), F32)], axis=0)
            part[slot] = found if start is None else found + start[slot]
            at += BLOCK


def pair_sums(v_parts, c_parts, v_starts, c_starts=()):
    v_count = 4 * len(v_parts)
    c_count = 4 * len(c_parts)
    extra = [start for start, _ in c_starts] + [start for start in v_starts if start is not None]
    args = [part for part, _ in [*v_parts, *c_parts]] + extra
    body = functools.partial(
        pair_kernel,
        max(1, UNROLL // v_count),
        [low for _, low in v_parts],
        [low for _, low in c_parts],
        [begin for _, begin in c_starts],
        [start is not None for start in v_starts],
    )
    outs = pl.pallas_call(
        body,
        out_shape=[jax.ShapeDtypeStruct((c_count, 56, BLOCK), F32)]
        + [jax.ShapeDtypeStruct((4, 8, BLOCK), F32)] * len(v_parts),
        in_specs=[pl.BlockSpec(memory_space=VMEM)] * len(args),
        out_specs=[pl.BlockSpec(memory_space=VMEM)] * (1 + len(v_parts)),
        scratch_shapes=[
            VMEM((WIDE, v_count * BLOCK), BF),
            VMEM((v_count * BLOCK, WIDE), BF),
            VMEM((c_count, WIDE, 2 * BLOCK), BF),
            VMEM((c_count, 16, BLOCK), BF),
            VMEM((16, v_count * BLOCK), F32),
        ],
        compiler_params=pltpu.CompilerParams(vmem_limit_bytes=48 * 2**20),
        cost_estimate=pl.CostEstimate(
            flops=v_count * c_count * 2 * 10**8, bytes_accessed=4 * 10**6, transcendentals=0
        ),
    )(*args)
    return outs


def swap(value, mask):
    return lax.ppermute(value, ("vol", "ctl"), [(i, i ^ mask) for i in range(256)])


def gather(value, masks):
    return jnp.concatenate([value] + [swap(value, mask) for mask in masks], axis=0)


def back(value, masks):
    return [swap(value[s + 1], mask) for s, mask in enumerate(masks)]


def tie(*values):
    return lax.optimization_barrier(values)


UNROLL = 8
X_MASKS = (4, 12, 8)
Y_MASKS = (64, 192, 128)
CORE, Z_ONE, Z_TWO, Z_SIX = (16, 1, 2, 34)


def shards(vol_coords, vol_cotangent, ctl_coords, ctl_weights):
    v, c = pack(vol_coords, vol_cotangent, ctl_coords, ctl_weights)
    cp, va = tie(gather(c, Y_MASKS), gather(v, X_MASKS))
    cq = swap(cp, CORE)
    cr = swap(cp, Z_ONE)
    vb = swap(va, Z_TWO)
    a = (va, 0)
    pq, sum_a = pair_sums([a], [(cp, 0), (cq, 0)], [None])
    cr, vb, pq = tie(cr, vb, pq)
    b = (vb, 0)
    v_far = swap(jnp.concatenate([va, vb], axis=0), Z_SIX)
    c, d = ((v_far, 0), (v_far, 4))
    cs = swap(cr, CORE)
    pqr, sum_b = pair_sums([b], [(cp, 0), (cq, 0), (cr, 0)], [None])
    s, sum_a, sum_b, sum_c, sum_d = pair_sums(
        [a, b, c, d], [(cs, 0)], [sum_a, sum_b, None, None]
    )
    s_back = swap(s, CORE)
    r, sum_a, sum_c, sum_d = pair_sums([a, c, d], [(cr, 0)], [sum_a, sum_c, sum_d], [(pqr, 8)])
    r = r + s_back
    r_back = swap(r, Z_ONE)
    r, pq = tie(r, pq)
    q, sum_c, sum_d = pair_sums([c, d], [(cq, 0)], [sum_c, sum_d], [(pq, 4), (pqr, 4)])
    q_back = swap(q, CORE)
    p, sum_d = pair_sums([d], [(cp, 0)], [sum_d], [(pq, 0), (pqr, 0)])
    bd_back = swap(jnp.concatenate([sum_b, sum_d], axis=0), Z_TWO)
    p, sum_c = pair_sums([c], [(cp, 0)], [sum_c], [(p, 0)])
    p, sum_c, bd_back, q_back, r_back = tie(p, sum_c, bd_back, q_back, r_back)
    p = p + q_back + r_back
    vol = sum_a + bd_back[:4] + swap(sum_c + bd_back[4:], Z_SIX)
    ctl, vol = tie([p[0], *back(p.astype(BF), Y_MASKS)], [vol[0], *back(vol, X_MASKS)])
    ctl = [term.astype(F32) for term in ctl]
    ctl = (ctl[0] + ctl[1]) + (ctl[2] + ctl[3])
    vol = (vol[0] + vol[1]) + (vol[2] + vol[3])
    return (ctl[0:48], vol[0:3], ctl[48:51])


def solution(mesh):
    in_specs = (
        P(None, ("vol", "ctl")),
        P(None, ("vol", "ctl")),
        P(None, ("ctl", "vol")),
        P(None, ("ctl", "vol")),
    )
    out_specs = (P(None, ("ctl", "vol")), P(None, ("vol", "ctl")), P(None, ("ctl", "vol")))
    return jax.shard_map(shards, mesh=mesh, in_specs=in_specs, out_specs=out_specs, check_vma=False)
```

```python
import functools

import jax
import jax.numpy as jnp
from jax import lax
from jax.experimental import pallas as pl
from jax.experimental.pallas import tpu as pltpu
from jax.sharding import PartitionSpec as P

F32 = jnp.float32
BF = jnp.bfloat16
VMEM = pltpu.VMEM
WIDE = 64
BLOCK = 256
SLOPE = -320.0


def split3(total):
    first = total.astype(BF)
    rest = total - first.astype(F32)
    second = rest.astype(BF)
    third = (rest - second.astype(F32)).astype(BF)
    return (first, second, third)


def pack_kernel(vx_ref, vc_ref, cx_ref, cw_ref, v_ref, c_ref):
    ones = jnp.ones((3, BLOCK), BF)
    blank = jnp.zeros((7, BLOCK), BF)
    v = vx_ref[...].astype(F32) * 4.0
    v_len = jnp.concatenate(split3(jnp.sum(v * v, axis=0, keepdims=True)), axis=0)
    v_ref[0, 0:48, :] = vc_ref[...]
    v_ref[0, 48:64, :] = jnp.concatenate([(v * -2.0).astype(BF), v_len, ones, blank], axis=0)
    c = cx_ref[...].astype(F32) * 4.0
    c_len = jnp.concatenate(split3(jnp.sum(c * c, axis=0, keepdims=True)), axis=0)
    c_ref[0, 0:48, :] = cw_ref[...]
    c_ref[0, 48:64, :] = jnp.concatenate([c.astype(BF), ones, c_len, blank], axis=0)


def pack(vol_coords, vol_cotangent, ctl_coords, ctl_weights):
    packed = jax.ShapeDtypeStruct((1, WIDE, BLOCK), BF)
    return pl.pallas_call(
        pack_kernel,
        out_shape=(packed, packed),
        in_specs=[pl.BlockSpec(memory_space=VMEM)] * 4,
        out_specs=[pl.BlockSpec(memory_space=VMEM)] * 2,
    )(vol_coords, vol_cotangent, ctl_coords, ctl_weights)


def pair_kernel(unroll, v_lows, c_lows, c_begins, v_begin, *refs):
    refs = list(refs)
    v_parts = [refs.pop(0) for _ in v_lows]
    c_parts = [refs.pop(0) for _ in c_lows]
    c_starts = [refs.pop(0) for _ in c_begins]
    v_starts = [refs.pop(0) if begin else None for begin in v_begin]
    c_out = refs.pop(0)
    v_outs = [refs.pop(0) for _ in v_lows]
    v_all, v_tall, c_two, c_pos, v_sum = refs
    at = 0
    for part, low in zip(v_parts, v_lows):
        for slot in range(4):
            block = part[low + slot]
            v_all[:, at : at + BLOCK] = block
            v_tall[at : at + BLOCK, :] = block.T
            at += BLOCK
    rows = lax.broadcasted_iota(jnp.int32, (WIDE, BLOCK), 0)
    count = 0
    for part, low in zip(c_parts, c_lows):
        for slot in range(4):
            block = part[low + slot]
            blank = jnp.zeros_like(block)
            c_two[count, :, :BLOCK] = jnp.where(rows >= 48, block, blank)
            c_two[count, :, BLOCK:] = jnp.where(rows < 48, block, blank)
            c_pos[count] = block[48:64]
            count += 1
    v_sum[...] = jnp.zeros_like(v_sum)

    def tile(n, carry):
        both = jnp.dot(v_tall[...], c_two[n], preferred_element_type=F32)
        squared = jnp.maximum(both[:, :BLOCK], 1e-20)
        pair_dot = both[:, BLOCK:]
        inside = jnp.maximum(1.0 - squared * lax.rsqrt(squared), 0.0)
        second = inside * inside
        kernel = (second * second * (inside - 1.25)).astype(BF)
        weighting = (second * inside * pair_dot).astype(BF)
        weight_grad = jnp.dot(v_all[0:48, :], kernel, preferred_element_type=F32)
        pushed = jnp.dot(v_all[48:64, :], weighting, preferred_element_type=F32)
        own = c_pos[n]
        v_sum[...] += lax.dot_general(
            own, weighting, (((1,), (1,)), ((), ())), preferred_element_type=F32
        )
        ctl_pos = own[0:3].astype(F32) * 0.25
        grad = (ctl_pos * pushed[6:7] + pushed[0:3] * 0.125) * SLOPE
        found = jnp.concatenate([weight_grad * -4.0, grad, jnp.zeros((5, BLOCK), F32)], axis=0)
        for start, begin in zip(c_starts, c_begins):
            found = found + start[begin + n]
        c_out[n] = found
        return carry

    lax.fori_loop(0, count, tile, 0, unroll=unroll)
    at = 0
    for part, start in zip(v_outs, v_starts):
        for slot in range(4):
            pulled = v_sum[:, at : at + BLOCK]
            vol_pos = v_all[48:64, at : at + BLOCK][0:3].astype(F32) * -0.125
            grad = (vol_pos * pulled[3:4] - pulled[0:3] * 0.25) * SLOPE
            found = jnp.concatenate([grad, jnp.zeros((5, BLOCK), F32)], axis=0)
            part[slot] = found if start is None else found + start[slot]
            at += BLOCK


def pair_sums(v_parts, c_parts, v_starts, c_starts=()):
    v_count = 4 * len(v_parts)
    c_count = 4 * len(c_parts)
    extra = [start for start, _ in c_starts] + [start for start in v_starts if start is not None]
    args = [part for part, _ in [*v_parts, *c_parts]] + extra
    body = functools.partial(
        pair_kernel,
        max(1, UNROLL // v_count),
        [low for _, low in v_parts],
        [low for _, low in c_parts],
        [begin for _, begin in c_starts],
        [start is not None for start in v_starts],
    )
    outs = pl.pallas_call(
        body,
        out_shape=[jax.ShapeDtypeStruct((c_count, 56, BLOCK), F32)]
        + [jax.ShapeDtypeStruct((4, 8, BLOCK), F32)] * len(v_parts),
        in_specs=[pl.BlockSpec(memory_space=VMEM)] * len(args),
        out_specs=[pl.BlockSpec(memory_space=VMEM)] * (1 + len(v_parts)),
        scratch_shapes=[
            VMEM((WIDE, v_count * BLOCK), BF),
            VMEM((v_count * BLOCK, WIDE), BF),
            VMEM((c_count, WIDE, 2 * BLOCK), BF),
            VMEM((c_count, 16, BLOCK), BF),
            VMEM((16, v_count * BLOCK), F32),
        ],
        compiler_params=pltpu.CompilerParams(vmem_limit_bytes=48 * 2**20),
        cost_estimate=pl.CostEstimate(
            flops=v_count * c_count * 2 * 10**8, bytes_accessed=4 * 10**6, transcendentals=0
        ),
    )(*args)
    return outs


def swap(value, mask):
    return lax.ppermute(value, ("vol", "ctl"), [(i, i ^ mask) for i in range(256)])


def gather(value, masks):
    return jnp.concatenate([value] + [swap(value, mask) for mask in masks], axis=0)


def back(value, masks):
    return [swap(value[s + 1], mask) for s, mask in enumerate(masks)]


def tie(*values):
    return lax.optimization_barrier(values)


UNROLL = 8
X_MASKS = (4, 12, 8)
Y_MASKS = (64, 192, 128)
CORE, Z_ONE, Z_TWO, Z_SIX = (16, 1, 2, 34)


def shards(vol_coords, vol_cotangent, ctl_coords, ctl_weights):
    v, c = pack(vol_coords, vol_cotangent, ctl_coords, ctl_weights)
    va, cp = tie(gather(v, X_MASKS), gather(c, Y_MASKS))
    vb = swap(va, Z_TWO)
    cq = swap(cp, CORE)
    cr = swap(cp, Z_ONE)
    a = (va, 0)
    pq, sum_a = pair_sums([a], [(cp, 0), (cq, 0)], [None])
    cr, vb, pq = tie(cr, vb, pq)
    b = (vb, 0)
    v_far = swap(jnp.concatenate([va, vb], axis=0), Z_SIX)
    c, d = ((v_far, 0), (v_far, 4))
    cs = swap(cr, CORE)
    pqr, sum_b = pair_sums([b], [(cp, 0), (cq, 0), (cr, 0)], [None])
    s, sum_a, sum_b, sum_c, sum_d = pair_sums(
        [a, b, c, d], [(cs, 0)], [sum_a, sum_b, None, None]
    )
    s_back = swap(s, CORE)
    r, sum_a, sum_c, sum_d = pair_sums([a, c, d], [(cr, 0)], [sum_a, sum_c, sum_d], [(pqr, 8)])
    r = r + s_back
    r_back = swap(r, Z_ONE)
    r, pq = tie(r, pq)
    q, sum_c, sum_d = pair_sums([c, d], [(cq, 0)], [sum_c, sum_d], [(pq, 4), (pqr, 4)])
    q_back = swap(q, CORE)
    p, sum_d = pair_sums([d], [(cp, 0)], [sum_d], [(pq, 0), (pqr, 0)])
    bd_back = swap(jnp.concatenate([sum_b, sum_d], axis=0), Z_TWO)
    p, sum_c = pair_sums([c], [(cp, 0)], [sum_c], [(p, 0)])
    p, sum_c, bd_back, q_back, r_back = tie(p, sum_c, bd_back, q_back, r_back)
    p = p + q_back + r_back
    vol = sum_a + bd_back[:4] + swap(sum_c + bd_back[4:], Z_SIX)
    ctl, vol = tie([p[0], *back(p.astype(BF), Y_MASKS)], [vol[0], *back(vol, X_MASKS)])
    ctl = [term.astype(F32) for term in ctl]
    ctl = (ctl[0] + ctl[1]) + (ctl[2] + ctl[3])
    vol = (vol[0] + vol[1]) + (vol[2] + vol[3])
    return (ctl[0:48], vol[0:3], ctl[48:51])


def solution(mesh):
    in_specs = (
        P(None, ("vol", "ctl")),
        P(None, ("vol", "ctl")),
        P(None, ("ctl", "vol")),
        P(None, ("ctl", "vol")),
    )
    out_specs = (P(None, ("ctl", "vol")), P(None, ("vol", "ctl")), P(None, ("ctl", "vol")))
    return jax.shard_map(shards, mesh=mesh, in_specs=in_specs, out_specs=out_specs, check_vma=False)
```
